128 devices in a mesh: blk: 16 (over z, x_lo, core), dp: 8 (over x_hi, y).
Axes of the slice: x: 4 (x_hi: 2, x_lo: 2; x = x_hi * 2 + x_lo), y: 4, z: 4, core: 2. Of those that a mesh axis runs over, the one named last changes fastest.
Arguments:
- inputs: bfloat16 [49152, 5120], P(('blk', 'dp')), may hold values from -6 to 6
- upstream: bfloat16 [49152, 5120], P(('blk', 'dp')), may hold values from -0.625 to 0.625
- norm_gain: float32 [5120], replicated, may hold values from 0.5 to 1.5
- gate_weight: bfloat16 [5120, 7168], P('dp', 'blk'), may hold values from -0.078125 to 0.078125
- up_weight: bfloat16 [5120, 7168], P('dp', 'blk'), may hold values from -0.078125 to 0.078125
- down_weight: bfloat16 [5120, 7168], P('dp', 'blk'), may hold values from -0.25 to 0.25
Outputs:
- layer_out: bfloat16 [49152, 5120], P(('blk', 'dp'))
- grad_input: bfloat16 [49152, 5120], P(('blk', 'dp'))
- grad_gate: bfloat16 [5120, 7168], P('dp', 'blk')
- grad_up: bfloat16 [5120, 7168], P('dp', 'blk')
- grad_down: bfloat16 [5120, 7168], P('dp', 'blk')
The draws below stay inside these ranges and needn't reach their ends.
All inputs are finite; a program needn't handle non-finite values.
Results may differ from the reference program's by a relative error of at most 0.015.
Values may be sent and summed in bfloat16 or wider, within the bound.
A program may use at most 128 MiB of HBM per device.

```python
import jax
import jax.numpy as jnp
from jax import lax

D = 5120
FF_BLK = 448
TOK_DEV = 384
FF = 7168
TOKENS = 49152
N_BLK = 16
N_DP = 8


def block_scale(key, extent, cuts, smallest, high):
    level = 1.0
    for axis_at, blocks in cuts:
        draws = jax.random.uniform(jax.random.fold_in(jax.random.fold_in(key, 6), axis_at), (blocks,), jnp.float32, smallest / len(cuts), high / len(cuts))
        level = level * jnp.repeat(jnp.exp(draws), extent[axis_at] // blocks).reshape((-1,) + (1,) * (len(extent) - 1 - axis_at))
    return level


def noise(rng, dims, width, bound, shards=(), kind=jnp.bfloat16):
    result = width * jax.random.normal(rng, dims, jnp.float32)
    if shards:
        result = result * block_scale(rng, dims, shards, -0.22, 0.18)
    return jnp.clip(result, -bound, bound).astype(kind)


def setup_inputs(seed: int = 0) -> dict:
    seeds = jax.random.split(jax.random.key(seed), 7)
    return {
        "inputs": noise(seeds[0], (TOKENS, D), 1.0, 6.0, ((0, 128),)),
        "upstream": noise(seeds[1], (TOKENS, D), 0.1, 0.625, ((0, 128),)),
        "norm_gain": jnp.clip(1.0 + 0.1 * jax.random.normal(seeds[2], (D,), jnp.float32), 0.5, 1.5),
        "gate_weight": noise(seeds[3], (D, FF), D ** -0.5, 0.078125, ((0, 8), (1, 16))),
        "up_weight": noise(seeds[4], (D, FF), D ** -0.5, 0.078125, ((0, 8), (1, 16))),
        "down_weight": noise(seeds[5], (D, FF), FF_BLK ** -0.5, 0.25, ((0, 8), (1, 16))),
    }


norm_eps = 1e-05

def contract_last(left_rows, right_rows):
    return lax.dot_general(left_rows, right_rows, (((1,), (1,)), ((), ())), preferred_element_type=jnp.float32)

def block_pass(rows_in, rows_cot, norm_gain, gate_block, up_block, down_block):
    wide_in = rows_in.astype(jnp.float32)
    inv_rms = lax.rsqrt(lax.optimization_barrier(jnp.mean(wide_in * wide_in, axis=-1, keepdims=True)) + norm_eps)
    normed = (wide_in * inv_rms * norm_gain).astype(jnp.bfloat16)
    gate_pre = jnp.dot(normed, gate_block, preferred_element_type=jnp.float32)
    up_pre = jnp.dot(normed, up_block, preferred_element_type=jnp.float32)
    sigmoid_gate = jax.nn.sigmoid(gate_pre)
    activated = gate_pre * sigmoid_gate
    hidden = (activated * up_pre).astype(jnp.bfloat16)
    layer_rows = (wide_in + contract_last(hidden, down_block)).astype(jnp.bfloat16)
    d_hidden = jnp.dot(rows_cot, down_block, preferred_element_type=jnp.float32)
    d_gate = (d_hidden * up_pre * sigmoid_gate * (1.0 + gate_pre * (1.0 - sigmoid_gate))).astype(jnp.bfloat16)
    d_up = (d_hidden * activated).astype(jnp.bfloat16)
    d_normed = contract_last(d_gate, gate_block) + contract_last(d_up, up_block)
    scaled_grad = d_normed * norm_gain
    along = lax.optimization_barrier(jnp.mean(scaled_grad * wide_in, axis=-1, keepdims=True))
    grad_rows = (rows_cot.astype(jnp.float32) + inv_rms * (scaled_grad - wide_in * inv_rms * inv_rms * along)).astype(jnp.bfloat16)
    return (layer_rows, grad_rows, normed, d_gate, d_up, hidden)

def device_sum(left_rows, right_rows):
    left_wide = left_rows.reshape(N_DP, TOK_DEV, left_rows.shape[-1]).astype(jnp.float32)
    right_wide = right_rows.reshape(N_DP, TOK_DEV, right_rows.shape[-1]).astype(jnp.float32)
    per_device = jnp.einsum('ntk,ntj->nkj', left_wide, right_wide)
    rounded = lax.optimization_barrier(per_device.astype(jnp.bfloat16))
    return lax.optimization_barrier(jnp.sum(rounded.astype(jnp.float32), axis=0))

def arrange(stacked):
    owned = jnp.roll(stacked, -1, axis=0)
    return jnp.transpose(owned, (1, 0, 2)).reshape(D, N_BLK * FF_BLK).astype(jnp.bfloat16)

def reference(inputs, upstream, norm_gain, gate_weight, up_weight, down_weight):
    group_rows = N_DP * TOK_DEV
    in_groups = inputs.reshape(N_BLK, group_rows, D)
    cot_groups = upstream.reshape(N_BLK, group_rows, D)

    def position(packed):
        cycle_pos, rows_in, rows_cot = packed
        first_col = ((cycle_pos + N_BLK - 1) % N_BLK * FF_BLK).astype(jnp.int32)
        gate_block = lax.dynamic_slice_in_dim(gate_weight, first_col, FF_BLK, 1)
        up_block = lax.dynamic_slice_in_dim(up_weight, first_col, FF_BLK, 1)
        down_block = lax.dynamic_slice_in_dim(down_weight, first_col, FF_BLK, 1)
        layer_rows, grad_rows, normed, d_gate, d_up, hidden = block_pass(rows_in, rows_cot, norm_gain, gate_block, up_block, down_block)
        return (layer_rows, grad_rows, device_sum(normed, d_gate), device_sum(normed, d_up), device_sum(rows_cot, hidden))
    per_position = lax.map(position, (jnp.arange(N_BLK, dtype=jnp.int32), in_groups, cot_groups))
    layer_out = per_position[0].reshape(N_BLK * group_rows, D)
    grad_input = per_position[1].reshape(N_BLK * group_rows, D)
    return (layer_out, grad_input, arrange(per_position[2]), arrange(per_position[3]), arrange(per_position[4]))
```

```python
import jax
import jax.numpy as jnp
from jax import lax
from jax.sharding import PartitionSpec as P

norm_eps = 1e-05


def shifted(value, axis, by):
    size = lax.axis_size(axis)
    return lax.ppermute(value, axis, [(i, (i + by) % size) for i in range(size)])


def contract_last(left_rows, right_rows):
    return lax.dot_general(
        left_rows, right_rows, (((1,), (1,)), ((), ())), preferred_element_type=jnp.float32
    )


def contract_first(left_rows, right_rows):
    return lax.dot_general(
        left_rows, right_rows, (((0,), (0,)), ((), ())), preferred_element_type=jnp.float32
    )


def block_pass(rows_in, rows_cot, norm_gain, gate_block, up_block, down_block):
    wide_in = rows_in.astype(jnp.float32)
    inv_rms = lax.rsqrt(jnp.mean(wide_in * wide_in, axis=-1, keepdims=True) + norm_eps)
    normed = (wide_in * inv_rms * norm_gain).astype(jnp.bfloat16)
    gate_pre = jnp.dot(normed, gate_block, preferred_element_type=jnp.float32)
    up_pre = jnp.dot(normed, up_block, preferred_element_type=jnp.float32)
    sigmoid_gate = jax.nn.sigmoid(gate_pre)
    activated = gate_pre * sigmoid_gate
    hidden = (activated * up_pre).astype(jnp.bfloat16)
    layer_rows = (wide_in + contract_last(hidden, down_block)).astype(jnp.bfloat16)
    d_hidden = jnp.dot(rows_cot, down_block, preferred_element_type=jnp.float32)
    d_gate = (d_hidden * up_pre * sigmoid_gate * (1.0 + gate_pre * (1.0 - sigmoid_gate))).astype(
        jnp.bfloat16
    )
    d_up = (d_hidden * activated).astype(jnp.bfloat16)
    d_normed = contract_last(d_gate, gate_block) + contract_last(d_up, up_block)
    scaled_grad = d_normed * norm_gain
    along = jnp.mean(scaled_grad * wide_in, axis=-1, keepdims=True)
    grad_rows = (
        rows_cot.astype(jnp.float32) + inv_rms * (scaled_grad - wide_in * inv_rms * inv_rms * along)
    ).astype(jnp.bfloat16)
    partials = (
        contract_first(normed, d_gate),
        contract_first(normed, d_up),
        contract_first(rows_cot, hidden),
    )
    return (layer_rows, grad_rows, partials)


def local(inputs, upstream, norm_gain, gate_weight, up_weight, down_weight):
    moved_gate, moved_up, moved_down = shifted((gate_weight, up_weight, down_weight), "blk", 1)
    gate_block, up_block, down_block = (
        lax.all_gather(moved_gate, "dp", axis=0, tiled=True),
        lax.all_gather(moved_up, "dp", axis=0, tiled=True),
        lax.all_gather(moved_down, "dp", axis=0, tiled=True),
    )
    layer_out, grad_input, partials = block_pass(
        inputs, upstream, norm_gain, gate_block, up_block, down_block
    )
    sums = tuple(
        lax.psum_scatter(p.astype(jnp.bfloat16), "dp", scatter_dimension=0, tiled=True)
        for p in partials
    )
    grad_gate, grad_up, grad_down = shifted(sums, "blk", -1)
    return (layer_out, grad_input, grad_gate, grad_up, grad_down)


def solution(mesh):
    placed = (
        P(("blk", "dp"), None),
        P(("blk", "dp"), None),
        P(),
        P("dp", "blk"),
        P("dp", "blk"),
        P("dp", "blk"),
    )
    return jax.shard_map(
        local,
        mesh=mesh,
        in_specs=placed,
        out_specs=(
            P(("blk", "dp"), None),
            P(("blk", "dp"), None),
            P("dp", "blk"),
            P("dp", "blk"),
            P("dp", "blk"),
        ),
        check_vma=False,
    )
```

```python
import functools

import jax
import jax.numpy as jnp
from jax import lax
from jax.experimental import pallas as pl
from jax.experimental.pallas import tpu as pltpu
from jax.sharding import PartitionSpec as P

norm_eps = 1e-05
MESH = pl.DeviceIdType.MESH
F32, BF16 = jnp.float32, jnp.bfloat16

CHUNK = {("a", 0): 0, ("b", 0): 1, ("a", 1): 2, ("b", 1): 3, ("a", 2): 4, ("b", 2): 5, ("a", 3): 6}
N_A, N_B, N_CHUNK = 4, 3, 7
SLOTS = 4
ORDER = (
    "a1.0 b1.0 b1.1 a1.1", "b1.2 a1.2 a2.0 b2.0", "b2.1 a1.3 a2.1 b2.2", "a2.2 a3.0 a2.3 b3.0",
    "a3.1 b3.1 a4.0 a4.1", "b3.2 b4.0 a5.0 a5.1", "b5.0 b4.1 b6.0 b5.1", "b6.1 b4.2 a3.2 b5.2",
    "a3.3 a6.0 a6.1 a4.2", "f.0 f.1 f.2 b6.2", "f.3 f.4 f.5 a4.3", "f.6 f.7 a5.2 a6.2",
    "a5.3 a6.3",
)


def nt(left, right):
    return lax.dot_general(left, right, (((1,), (1,)), ((), ())), preferred_element_type=F32)


def kernel(
    n_blk, x_any, up_any, gain_ref, own, lo_any, gi_any, g_ref,
    xin, up, normed, inv, wt, part, stage, rc1, rb1, ra1, ra2, rc2, rb2,
    hid_t, dg_t, du_t, hid, dg, du, along_t, along, ss, rs, ls,
):
    tok, width = xin.shape
    ff = wt.shape[1]
    ch = ff // N_CHUNK
    half = ch // 2
    sh = width // 8

    blk, dp = lax.axis_index("blk"), lax.axis_index("dp")
    xh, y = dp // 4, dp % 4
    nxt, prv = lax.rem(blk + 1, n_blk), lax.rem(blk + n_blk - 1, n_blk)
    yu, yd, yo = lax.rem(y + 1, 4), lax.rem(y + 3, 4), lax.rem(y + 2, 4)
    xo = 1 - xh
    up_dev, dn_dev = (blk, xh * 4 + yu), (blk, xh * 4 + yd)
    to_blk = ((nxt, dp), (nxt, xo * 4 + y))
    back_blk = ((prv, dp), (prv, xo * 4 + y))

    def lanes(owner, count=1):
        return pl.ds(pl.multiple_of(owner * sh, 128), count * sh)

    counter = [0]
    live = {}

    def send(name, src, dst, target):
        i = counter[0]
        counter[0] += 1
        cp = pltpu.make_async_remote_copy(
            src_ref=src, dst_ref=dst, send_sem=ss.at[i], recv_sem=rs.at[i],
            device_id=target, device_id_type=MESH,
        )
        cp.start()
        live.setdefault(name, []).append(cp)

    waited = set()

    def arrived(name):
        for cp in live[name]:
            cp.wait_recv()

    def sent(name):
        for cp in live[name]:
            cp.wait_send()
        waited.add(name)

    load_x = pltpu.make_async_copy(x_any, xin, ls.at[0])
    load_u = pltpu.make_async_copy(up_any, up, ls.at[1])
    load_x.start()
    load_u.start()

    barrier = pltpu.get_barrier_semaphore()
    for other in (up_dev, dn_dev) + to_blk + back_blk:
        pl.semaphore_signal(barrier, inc=1, device_id=other, device_id_type=MESH)
    pl.semaphore_wait(barrier, 6)

    def rows(c):
        return pl.ds(c * ch, ch)

    lo_half, hi_half = pl.ds(0, half), pl.ds(half, half)

    for j in range(max(N_A, N_B)):
        if j < N_A:
            c = CHUNK["a", j]
            for k in range(2):
                send(("A1", j), own.at[:, rows(c)], wt.at[:, rows(c), lanes(dp)], to_blk[k])
        if j < N_B:
            c = CHUNK["b", j]
            send(("B2", j), own.at[:, rows(c)], stage.at[j, 0], up_dev)
            send(("B2", j), own.at[:, rows(c)], stage.at[j, 1], dn_dev)
            for k in range(2):
                send(("A2", j), own.at[:, rows(c)], wt.at[:, rows(c), lanes(dp)], to_blk[k])

    load_x.wait()

    @pl.loop(0, tok // 16)
    def _(r):
        at = pl.ds(pl.multiple_of(r * 16, 16), 16)
        wide = xin[at, :].astype(F32)
        scale = lax.rsqrt(jnp.mean(wide * wide, axis=-1, keepdims=True) + norm_eps)
        inv[at, :] = jnp.broadcast_to(scale, (16, 128))
        normed[at, :] = (wide * scale * gain_ref[...]).astype(BF16)

    along_t[...] = jnp.zeros_like(along_t)
    load_u.wait()

    def compute(c):
        slot = c % SLOTS
        both = jnp.concatenate([wt[0, rows(c), :], wt[1, rows(c), :]], axis=0)
        pre = nt(both, normed[...])
        d_hidden = nt(wt[2, rows(c), :], up[...])
        gate, upp = pre[:ch], pre[ch:]
        sig = jax.nn.sigmoid(gate)
        act = gate * sig
        hidden = (act * upp).astype(BF16)
        d_gate = (d_hidden * upp * sig * (1.0 + gate * (1.0 - sig))).astype(BF16)
        d_up = (d_hidden * act).astype(BF16)
        hid_t[rows(c), :] = hidden
        dg_t[rows(c), :] = d_gate
        du_t[rows(c), :] = d_up
        summed = d_gate.astype(F32) * gate + d_up.astype(F32) * upp
        along_t[...] += jnp.broadcast_to(jnp.sum(summed, axis=0, keepdims=True), along_t.shape)

        @pl.loop(0, 8)
        def _(o):
            at = lanes(o)
            gu = jnp.concatenate([dg_t[rows(c), :], du_t[rows(c), :]], axis=0)
            pair = jnp.dot(gu, normed[:, at], preferred_element_type=F32)
            part[slot, 0, :, at] = pair[:ch].astype(BF16)
            part[slot, 1, :, at] = pair[ch:].astype(BF16)
            part[slot, 2, :, at] = jnp.dot(
                hid_t[rows(c), :], up[:, at], preferred_element_type=F32
            ).astype(BF16)

    def add(out, *terms):
        for w in range(3):
            total = terms[0][w].astype(F32)
            for term in terms[1:]:
                total = total + term[w].astype(F32)
            out[w] = total.astype(BF16)

    def reuse(c):
        if c >= SLOTS:
            old = {v: k for k, v in CHUNK.items()}[c - SLOTS]
            for name in ("c1", "b1", "a1") if old[0] == "a" else ("a2",):
                sent((name, old[1]))

    def a1(j, c):
        arrived(("A1", j))
        for x in range(2):
            at = lanes(4 * x + y)
            send(("B1", j), wt.at[:, rows(c), at], wt.at[:, rows(c), at], up_dev)
            send(("B1", j), wt.at[:, rows(c), at], wt.at[:, rows(c), at], dn_dev)

    def a2(j, c):
        arrived(("B1", j))
        low, high = pl.ds(c * ch, half), pl.ds(c * ch + half, half)
        for x in range(2):
            at = lanes(4 * x + yd)
            send(("C1", j), wt.at[:, low, at], wt.at[:, low, at], up_dev)
            at = lanes(4 * x + yu)
            send(("C1", j), wt.at[:, high, at], wt.at[:, high, at], dn_dev)

    def a3(j, c):
        arrived(("C1", j))
        reuse(c)
        compute(c)
        slot = c % SLOTS
        for x in range(2):
            at = lanes(4 * x + yo)
            send(("c1", j), part.at[slot, :, lo_half, at], rc1.at[j, 0, x], up_dev)
            send(("c1", j), part.at[slot, :, hi_half, at], rc1.at[j, 1, x], dn_dev)

    def a4(j, c):
        arrived(("c1", j))
        slot = c % SLOTS
        for x in range(2):
            at = lanes(4 * x + yu)
            mine = part.at[slot, :, lo_half, at]
            add(mine, mine, rc1.at[j, 0, x])
            send(("b1", j), part.at[slot, :, :, at], rb1.at[j, 0, x], up_dev)
            at = lanes(4 * x + yd)
            mine = part.at[slot, :, hi_half, at]
            add(mine, mine, rc1.at[j, 1, x])
            send(("b1", j), part.at[slot, :, :, at], rb1.at[j, 1, x], dn_dev)

    def a5(j, c):
        arrived(("b1", j))
        slot = c % SLOTS
        for x in range(2):
            mine = part.at[slot, :, :, lanes(4 * x + y)]
            add(mine, mine, rb1.at[j, 0, x], rb1.at[j, 1, x])
        for k in range(2):
            at = lanes(4 * (xh if k == 0 else xo) + y)
            send(("a1", j), part.at[slot, :, :, at], ra1.at[j, k], back_blk[k])

    def a6(j, c):
        arrived(("a1", j))
        add(g_ref.at[:, rows(c)], ra1.at[j, 0], ra1.at[j, 1])

    def b1(j, c):
        arrived(("B2", j))
        send(("C2", j), stage.at[j, 0, :, lo_half], stage.at[j, 2, :, lo_half], up_dev)
        send(("C2", j), stage.at[j, 1, :, hi_half], stage.at[j, 2, :, hi_half], dn_dev)
        for s, yy in ((0, yd), (1, yu)):
            for k in range(2):
                send(("A2", j), stage.at[j, s], wt.at[:, rows(c), lanes(xh * 4 + yy)], to_blk[k])

    def b2(j, c):
        arrived(("C2", j))
        for k in range(2):
            send(("A2", j), stage.at[j, 2], wt.at[:, rows(c), lanes(xh * 4 + yo)], to_blk[k])

    def b3(j, c):
        arrived(("A2", j))
        reuse(c)
        compute(c)
        slot = c % SLOTS
        for k in range(2):
            at = lanes(4 * (xh if k == 0 else xo), 4)
            send(("a2", j), part.at[slot, :, :, at], ra2.at[j, k], back_blk[k])

    def b4(j, c):
        arrived(("a2", j))
        add(ra2.at[j, 0], ra2.at[j, 0], ra2.at[j, 1])
        send(("c2", j), ra2.at[j, 0, :, lo_half, lanes(yo)], rc2.at[j, 0], up_dev)
        send(("c2", j), ra2.at[j, 0, :, hi_half, lanes(yo)], rc2.at[j, 1], dn_dev)

    def b5(j, c):
        arrived(("c2", j))
        mine = ra2.at[j, 0, :, lo_half, lanes(yu)]
        add(mine, mine, rc2.at[j, 0])
        send(("b2", j), ra2.at[j, 0, :, :, lanes(yu)], rb2.at[j, 0], up_dev)
        mine = ra2.at[j, 0, :, hi_half, lanes(yd)]
        add(mine, mine, rc2.at[j, 1])
        send(("b2", j), ra2.at[j, 0, :, :, lanes(yd)], rb2.at[j, 1], dn_dev)

    def b6(j, c):
        arrived(("b2", j))
        add(g_ref.at[:, rows(c)], ra2.at[j, 0, :, :, lanes(y)], rb2.at[j, 0], rb2.at[j, 1])

    stores = []

    def f(t):
        if t == 0:
            hid[...] = hid_t[...].T
            dg[...] = dg_t[...].T
            du[...] = du_t[...].T
            along[...] = along_t[...].T / (inv[...] * width)
        at = lanes(t)
        scale = inv[:, :1]
        wide = xin[:, at].astype(F32)
        out = jnp.dot(hid[...], wt[2, :, at], preferred_element_type=F32)
        normed[:, at] = (wide + out).astype(BF16)
        cp = pltpu.make_async_copy(normed.at[:, at], lo_any.at[:, at], ls.at[2 + 2 * t])
        cp.start()
        stores.append(cp)
        d_normed = jnp.dot(dg[...], wt[0, :, at], preferred_element_type=F32)
        d_normed = d_normed + jnp.dot(du[...], wt[1, :, at], preferred_element_type=F32)
        scaled = d_normed * gain_ref[:, at]
        grad = up[:, at].astype(F32) + scale * (scaled - wide * scale * scale * along[:, :1])
        up[:, at] = grad.astype(BF16)
        cp = pltpu.make_async_copy(up.at[:, at], gi_any.at[:, at], ls.at[3 + 2 * t])
        cp.start()
        stores.append(cp)

    table = {"a1": a1, "a2": a2, "a3": a3, "a4": a4, "a5": a5, "a6": a6,
             "b1": b1, "b2": b2, "b3": b3, "b4": b4, "b5": b5, "b6": b6}
    for line in ORDER:
        for task in line.split():
            kind, j = task.split(".")
            if kind == "f":
                f(int(j))
            else:
                table[kind](int(j), CHUNK[kind[0], int(j)])

    for cp in stores:
        cp.wait()
    for name in live:
        if name not in waited:
            sent(name)


N_COPIES = N_A * (2 + 4 + 4 + 4 + 4 + 2) + N_B * (2 + 2 + 8 + 2 + 2 + 2)


def solution(mesh):
    n_blk = mesh.shape["blk"]

    def local(inputs, upstream, norm_gain, gate_weight, up_weight, down_weight):
        tok, width = inputs.shape
        sh, ff = gate_weight.shape
        ch = ff // N_CHUNK
        own = jnp.stack([gate_weight.T, up_weight.T, down_weight.T])
        hbm = pl.BlockSpec(memory_space=pltpu.HBM)
        vmem = pl.BlockSpec(memory_space=pltpu.VMEM)
        flops = 9 * 2 * tok * width * ff
        lo, gi, g = pl.pallas_call(
            functools.partial(kernel, n_blk),
            name="ring",
            out_shape=(
                jax.ShapeDtypeStruct((tok, width), BF16),
                jax.ShapeDtypeStruct((tok, width), BF16),
                jax.ShapeDtypeStruct((3, ff, sh), BF16),
            ),
            in_specs=[hbm, hbm, vmem, hbm],
            out_specs=(hbm, hbm, vmem),
            scratch_shapes=[
                pltpu.VMEM((tok, width), BF16),
                pltpu.VMEM((tok, width), BF16),
                pltpu.VMEM((tok, width), BF16),
                pltpu.VMEM((tok, 128), F32),
                pltpu.VMEM((3, ff, width), BF16),
                pltpu.VMEM((SLOTS, 3, ch, width), BF16),
                pltpu.VMEM((N_B, 3, 3, ch, sh), BF16),
                pltpu.VMEM((N_A, 2, 2, 3, ch // 2, sh), BF16),
                pltpu.VMEM((N_A, 2, 2, 3, ch, sh), BF16),
                pltpu.VMEM((N_A, 2, 3, ch, sh), BF16),
                pltpu.VMEM((N_B, 2, 3, ch, 4 * sh), BF16),
                pltpu.VMEM((N_B, 2, 3, ch // 2, sh), BF16),
                pltpu.VMEM((N_B, 2, 3, ch, sh), BF16),
                pltpu.VMEM((ff, tok), BF16),
                pltpu.VMEM((ff, tok), BF16),
                pltpu.VMEM((ff, tok), BF16),
                pltpu.VMEM((tok, ff), BF16),
                pltpu.VMEM((tok, ff), BF16),
                pltpu.VMEM((tok, ff), BF16),
                pltpu.VMEM((128, tok), F32),
                pltpu.VMEM((tok, 128), F32),
                pltpu.SemaphoreType.DMA((N_COPIES,)),
                pltpu.SemaphoreType.DMA((N_COPIES,)),
                pltpu.SemaphoreType.DMA((18,)),
            ],
            compiler_params=pltpu.CompilerParams(
                collective_id=0, has_side_effects=True, vmem_limit_bytes=63 * 2**20
            ),
            cost_estimate=pl.CostEstimate(
                flops=flops, bytes_accessed=8 * tok * width, transcendentals=tok * ff
            ),
        )(inputs, upstream, norm_gain.reshape(1, width), own)
        return (lo, gi, g[0].T, g[1].T, g[2].T)

    tokens, weights = P(("blk", "dp"), None), P("dp", "blk")
    return jax.shard_map(
        local,
        mesh=mesh,
        in_specs=(tokens, tokens, P(), weights, weights, weights),
        out_specs=(tokens, tokens, weights, weights, weights),
        check_vma=False,
    )
```

```python
import functools

import jax
import jax.numpy as jnp
from jax import lax
from jax.experimental import pallas as pl
from jax.experimental.pallas import tpu as pltpu
from jax.sharding import PartitionSpec as P

norm_eps = 1e-05
MESH = pl.DeviceIdType.MESH
F32, BF16 = jnp.float32, jnp.bfloat16

CHUNK = {("a", 0): 0, ("b", 0): 1, ("a", 1): 2, ("b", 1): 3, ("a", 2): 4, ("b", 2): 5, ("a", 3): 6}
N_A, N_B, N_CHUNK = 4, 3, 7
SLOTS = 5
ORDER = (
    "a1.0 b1.0 b1.1 a1.1", "b1.2 a1.2 a2.0 b2.0", "b2.1 a1.3 a2.1 b2.2", "a2.2 a3.0 a2.3 b3.0",
    "a3.1 b3.1 a4.0 a3.2", "a4.1 a3.3 b4.0 a5.0", "a4.2 a5.1 b4.1 a4.3", "b3.2 b5.0 a6.0 a6.1",
    "f.0 f.1 f.2 a5.2", "f.3 b5.1 f.4 f.5", "f.6 f.7 a5.3 b4.2", "b6.0 a6.2 b6.1 b5.2",
    "a6.3 b6.2",
)


def nt(left, right):
    return lax.dot_general(left, right, (((1,), (1,)), ((), ())), preferred_element_type=F32)


def kernel(
    n_blk, x_any, up_any, gain_ref, own, lo_any, gi_any, g_ref,
    xin, up, normed, inv, wt, part, stage, rc1, rb1, ra1, ra2, rc2, rb2,
    hid_t, dg_t, du_t, hid, dg, du, along_t, along, ss, rs, ls,
):
    tok, width = xin.shape
    ff = wt.shape[1]
    ch = ff // N_CHUNK
    half = ch // 2
    sh = width // 8

    blk, dp = lax.axis_index("blk"), lax.axis_index("dp")
    xh, y = dp // 4, dp % 4
    nxt, prv = lax.rem(blk + 1, n_blk), lax.rem(blk + n_blk - 1, n_blk)
    yu, yd, yo = lax.rem(y + 1, 4), lax.rem(y + 3, 4), lax.rem(y + 2, 4)
    xo = 1 - xh
    up_dev, dn_dev = (blk, xh * 4 + yu), (blk, xh * 4 + yd)
    to_blk = ((nxt, dp), (nxt, xo * 4 + y))
    back_blk = ((prv, dp), (prv, xo * 4 + y))

    def lanes(owner, count=1):
        return pl.ds(pl.multiple_of(owner * sh, 128), count * sh)

    counter = [0]
    live = {}

    def send(name, src, dst, target):
        i = counter[0]
        counter[0] += 1
        cp = pltpu.make_async_remote_copy(
            src_ref=src, dst_ref=dst, send_sem=ss.at[i], recv_sem=rs.at[i],
            device_id=target, device_id_type=MESH,
        )
        cp.start()
        live.setdefault(name, []).append(cp)

    waited = set()

    def arrived(name):
        for cp in live[name]:
            cp.wait_recv()

    def sent(name):
        for cp in live[name]:
            cp.wait_send()
        waited.add(name)

    load_x = pltpu.make_async_copy(x_any, xin, ls.at[0])
    load_u = pltpu.make_async_copy(up_any, up, ls.at[1])
    load_x.start()
    load_u.start()

    barrier = pltpu.get_barrier_semaphore()
    for other in (up_dev, dn_dev) + to_blk + back_blk:
        pl.semaphore_signal(barrier, inc=1, device_id=other, device_id_type=MESH)
    pl.semaphore_wait(barrier, 6)

    def rows(c):
        return pl.ds(c * ch, ch)

    lo_half, hi_half = pl.ds(0, half), pl.ds(half, half)

    for j in range(max(N_A, N_B)):
        if j < N_A:
            c = CHUNK["a", j]
            for k in range(2):
                send(("A1", j), own.at[:, rows(c)], wt.at[:, rows(c), lanes(dp)], to_blk[k])
        if j < N_B:
            c = CHUNK["b", j]
            send(("B2", j), own.at[:, rows(c)], stage.at[j, 0], up_dev)
            send(("B2", j), own.at[:, rows(c)], stage.at[j, 1], dn_dev)
            for k in range(2):
                send(("A2", j), own.at[:, rows(c)], wt.at[:, rows(c), lanes(dp)], to_blk[k])

    load_x.wait()

    @pl.loop(0, tok // 16)
    def _(r):
        at = pl.ds(pl.multiple_of(r * 16, 16), 16)
        wide = xin[at, :].astype(F32)
        scale = lax.rsqrt(jnp.mean(wide * wide, axis=-1, keepdims=True) + norm_eps)
        inv[at, :] = jnp.broadcast_to(scale, (16, 128))
        normed[at, :] = (wide * scale * gain_ref[...]).astype(BF16)

    along_t[...] = jnp.zeros_like(along_t)
    load_u.wait()

    def compute(c):
        slot = c % SLOTS
        both = jnp.concatenate([wt[0, rows(c), :], wt[1, rows(c), :]], axis=0)
        pre = nt(both, normed[...])
        d_hidden = nt(wt[2, rows(c), :], up[...])
        gate, upp = pre[:ch], pre[ch:]
        sig = jax.nn.sigmoid(gate)
        act = gate * sig
        hidden = (act * upp).astype(BF16)
        d_gate = (d_hidden * upp * sig * (1.0 + gate * (1.0 - sig))).astype(BF16)
        d_up = (d_hidden * act).astype(BF16)
        hid_t[rows(c), :] = hidden
        dg_t[rows(c), :] = d_gate
        du_t[rows(c), :] = d_up
        summed = d_gate.astype(F32) * gate + d_up.astype(F32) * upp
        along_t[...] += jnp.broadcast_to(jnp.sum(summed, axis=0, keepdims=True), along_t.shape)

        @pl.loop(0, 8)
        def _(o):
            at = lanes(o)
            gu = jnp.concatenate([dg_t[rows(c), :], du_t[rows(c), :]], axis=0)
            pair = jnp.dot(gu, normed[:, at], preferred_element_type=F32)
            part[slot, 0, :, at] = pair[:ch].astype(BF16)
            part[slot, 1, :, at] = pair[ch:].astype(BF16)
            part[slot, 2, :, at] = jnp.dot(
                hid_t[rows(c), :], up[:, at], preferred_element_type=F32
            ).astype(BF16)

    def add(out, *terms):
        for w in range(3):
            total = terms[0][w].astype(F32)
            for term in terms[1:]:
                total = total + term[w].astype(F32)
            out[w] = total.astype(BF16)

    def reuse(c):
        if c >= SLOTS:
            old = {v: k for k, v in CHUNK.items()}[c - SLOTS]
            for name in ("c1", "b1", "a1") if old[0] == "a" else ("a2",):
                sent((name, old[1]))

    def a1(j, c):
        arrived(("A1", j))
        for x in range(2):
            at = lanes(4 * x + y)
            send(("B1", j), wt.at[:, rows(c), at], wt.at[:, rows(c), at], up_dev)
            send(("B1", j), wt.at[:, rows(c), at], wt.at[:, rows(c), at], dn_dev)

    def a2(j, c):
        arrived(("B1", j))
        low, high = pl.ds(c * ch, half), pl.ds(c * ch + half, half)
        for x in range(2):
            at = lanes(4 * x + yd)
            send(("C1", j), wt.at[:, low, at], wt.at[:, low, at], up_dev)
            at = lanes(4 * x + yu)
            send(("C1", j), wt.at[:, high, at], wt.at[:, high, at], dn_dev)

    def a3(j, c):
        arrived(("C1", j))
        reuse(c)
        compute(c)
        slot = c % SLOTS
        for x in range(2):
            at = lanes(4 * x + yo)
            send(("c1", j), part.at[slot, :, lo_half, at], rc1.at[j, 0, x], up_dev)
            send(("c1", j), part.at[slot, :, hi_half, at], rc1.at[j, 1, x], dn_dev)

    def a4(j, c):
        arrived(("c1", j))
        slot = c % SLOTS
        for x in range(2):
            at = lanes(4 * x + yu)
            mine = part.at[slot, :, lo_half, at]
            add(mine, mine, rc1.at[j, 0, x])
            send(("b1", j), part.at[slot, :, :, at], rb1.at[j, 0, x], up_dev)
            at = lanes(4 * x + yd)
            mine = part.at[slot, :, hi_half, at]
            add(mine, mine, rc1.at[j, 1, x])
            send(("b1", j), part.at[slot, :, :, at], rb1.at[j, 1, x], dn_dev)

    def a5(j, c):
        arrived(("b1", j))
        slot = c % SLOTS
        for x in range(2):
            mine = part.at[slot, :, :, lanes(4 * x + y)]
            add(mine, mine, rb1.at[j, 0, x], rb1.at[j, 1, x])
        for k in range(2):
            at = lanes(4 * (xh if k == 0 else xo) + y)
            send(("a1", j), part.at[slot, :, :, at], ra1.at[j, k], back_blk[k])

    def a6(j, c):
        arrived(("a1", j))
        add(g_ref.at[:, rows(c)], ra1.at[j, 0], ra1.at[j, 1])

    def b1(j, c):
        arrived(("B2", j))
        send(("C2", j), stage.at[j, 0, :, lo_half], stage.at[j, 2, :, lo_half], up_dev)
        send(("C2", j), stage.at[j, 1, :, hi_half], stage.at[j, 2, :, hi_half], dn_dev)
        for s, yy in ((0, yd), (1, yu)):
            for k in range(2):
                send(("A2", j), stage.at[j, s], wt.at[:, rows(c), lanes(xh * 4 + yy)], to_blk[k])

    def b2(j, c):
        arrived(("C2", j))
        for k in range(2):
            send(("A2", j), stage.at[j, 2], wt.at[:, rows(c), lanes(xh * 4 + yo)], to_blk[k])

    def b3(j, c):
        arrived(("A2", j))
        reuse(c)
        compute(c)
        slot = c % SLOTS
        for k in range(2):
            at = lanes(4 * (xh if k == 0 else xo), 4)
            send(("a2", j), part.at[slot, :, :, at], ra2.at[j, k], back_blk[k])

    def b4(j, c):
        arrived(("a2", j))
        add(ra2.at[j, 0], ra2.at[j, 0], ra2.at[j, 1])
        send(("c2", j), ra2.at[j, 0, :, lo_half, lanes(yo)], rc2.at[j, 0], up_dev)
        send(("c2", j), ra2.at[j, 0, :, hi_half, lanes(yo)], rc2.at[j, 1], dn_dev)

    def b5(j, c):
        arrived(("c2", j))
        mine = ra2.at[j, 0, :, lo_half, lanes(yu)]
        add(mine, mine, rc2.at[j, 0])
        send(("b2", j), ra2.at[j, 0, :, :, lanes(yu)], rb2.at[j, 0], up_dev)
        mine = ra2.at[j, 0, :, hi_half, lanes(yd)]
        add(mine, mine, rc2.at[j, 1])
        send(("b2", j), ra2.at[j, 0, :, :, lanes(yd)], rb2.at[j, 1], dn_dev)

    def b6(j, c):
        arrived(("b2", j))
        add(g_ref.at[:, rows(c)], ra2.at[j, 0, :, :, lanes(y)], rb2.at[j, 0], rb2.at[j, 1])

    stores = []

    def f(t):
        if t == 0:
            hid[...] = hid_t[...].T
            dg[...] = dg_t[...].T
            du[...] = du_t[...].T
            along[...] = along_t[...].T / (inv[...] * width)
        at = lanes(t)
        scale = inv[:, :1]
        wide = xin[:, at].astype(F32)
        out = jnp.dot(hid[...], wt[2, :, at], preferred_element_type=F32)
        normed[:, at] = (wide + out).astype(BF16)
        cp = pltpu.make_async_copy(normed.at[:, at], lo_any.at[:, at], ls.at[2 + 2 * t])
        cp.start()
        stores.append(cp)
        d_normed = jnp.dot(dg[...], wt[0, :, at], preferred_element_type=F32)
        d_normed = d_normed + jnp.dot(du[...], wt[1, :, at], preferred_element_type=F32)
        scaled = d_normed * gain_ref[:, at]
        grad = up[:, at].astype(F32) + scale * (scaled - wide * scale * scale * along[:, :1])
        up[:, at] = grad.astype(BF16)
        cp = pltpu.make_async_copy(up.at[:, at], gi_any.at[:, at], ls.at[3 + 2 * t])
        cp.start()
        stores.append(cp)

    table = {"a1": a1, "a2": a2, "a3": a3, "a4": a4, "a5": a5, "a6": a6,
             "b1": b1, "b2": b2, "b3": b3, "b4": b4, "b5": b5, "b6": b6}
    for line in ORDER:
        for task in line.split():
            kind, j = task.split(".")
            if kind == "f":
                f(int(j))
            else:
                table[kind](int(j), CHUNK[kind[0], int(j)])

    for cp in stores:
        cp.wait()
    for name in live:
        if name not in waited:
            sent(name)


N_COPIES = N_A * (2 + 4 + 4 + 4 + 4 + 2) + N_B * (2 + 2 + 8 + 2 + 2 + 2)


def solution(mesh):
    n_blk = mesh.shape["blk"]

    def local(inputs, upstream, norm_gain, gate_weight, up_weight, down_weight):
        tok, width = inputs.shape
        sh, ff = gate_weight.shape
        ch = ff // N_CHUNK
        own = jnp.stack([gate_weight.T, up_weight.T, down_weight.T])
        hbm = pl.BlockSpec(memory_space=pltpu.HBM)
        vmem = pl.BlockSpec(memory_space=pltpu.VMEM)
        flops = 9 * 2 * tok * width * ff
        lo, gi, g = pl.pallas_call(
            functools.partial(kernel, n_blk),
            name="ring",
            out_shape=(
                jax.ShapeDtypeStruct((tok, width), BF16),
                jax.ShapeDtypeStruct((tok, width), BF16),
                jax.ShapeDtypeStruct((3, ff, sh), BF16),
            ),
            in_specs=[hbm, hbm, vmem, hbm],
            out_specs=(hbm, hbm, vmem),
            scratch_shapes=[
                pltpu.VMEM((tok, width), BF16),
                pltpu.VMEM((tok, width), BF16),
                pltpu.VMEM((tok, width), BF16),
                pltpu.VMEM((tok, 128), F32),
                pltpu.VMEM((3, ff, width), BF16),
                pltpu.VMEM((SLOTS, 3, ch, width), BF16),
                pltpu.VMEM((N_B, 3, 3, ch, sh), BF16),
                pltpu.VMEM((N_A, 2, 2, 3, ch // 2, sh), BF16),
                pltpu.VMEM((N_A, 2, 2, 3, ch, sh), BF16),
                pltpu.VMEM((N_A, 2, 3, ch, sh), BF16),
                pltpu.VMEM((N_B, 2, 3, ch, 4 * sh), BF16),
                pltpu.VMEM((N_B, 2, 3, ch // 2, sh), BF16),
                pltpu.VMEM((N_B, 2, 3, ch, sh), BF16),
                pltpu.VMEM((ff, tok), BF16),
                pltpu.VMEM((ff, tok), BF16),
                pltpu.VMEM((ff, tok), BF16),
                pltpu.VMEM((tok, ff), BF16),
                pltpu.VMEM((tok, ff), BF16),
                pltpu.VMEM((tok, ff), BF16),
                pltpu.VMEM((128, tok), F32),
                pltpu.VMEM((tok, 128), F32),
                pltpu.SemaphoreType.DMA((N_COPIES,)),
                pltpu.SemaphoreType.DMA((N_COPIES,)),
                pltpu.SemaphoreType.DMA((18,)),
            ],
            compiler_params=pltpu.CompilerParams(
                collective_id=0, has_side_effects=True, vmem_limit_bytes=63 * 2**20
            ),
            cost_estimate=pl.CostEstimate(
                flops=flops, bytes_accessed=8 * tok * width, transcendentals=tok * ff
            ),
        )(inputs, upstream, norm_gain.reshape(1, width), own)
        return (lo, gi, g[0].T, g[1].T, g[2].T)

    tokens, weights = P(("blk", "dp"), None), P("dp", "blk")
    return jax.shard_map(
        local,
        mesh=mesh,
        in_specs=(tokens, tokens, P(), weights, weights, weights),
        out_specs=(tokens, tokens, weights, weights, weights),
        check_vma=False,
    )
```
